32 devices in a mesh: dp: 16 (over z, x, core), tensor: 2 (over y).
Axes of the slice: x: 2, y: 2, z: 4, core: 2. Of those that a mesh axis runs over, the one named last changes fastest.
Arguments:
- master: float32 [2, 16384, 16384], P(None, ('tensor', 'dp')), may hold values from -0.09375 to 0.09375
- tile_order: int32 [2, 64], P('tensor'), may hold values from 0 to 63, each once within a row
- check_weights: int32 [8, 16384], P(None, 'tensor'), may hold values from -7 to 7
Outputs:
- tiled: bfloat16 [2, 16384, 16384], P(None, 'tensor', 'dp')
- checksum: float32 [2, 8, 16384], P(None, None, ('dp', 'tensor'))
The draws below stay inside these ranges and needn't reach their ends.
Inputs may be any that keep to these rules, and one draw needn't show every extreme that they name: Each row of tile_order lists every number of 0 to 63 once.
All inputs are finite; a program needn't handle non-finite values.
Results may differ from the reference program's by a relative error of at most 0.0029.
Values may be sent and summed in bfloat16 or wider, within the bound.
A program may use at most 192 MiB of HBM per device.

```python
import jax
import jax.numpy as jnp

D = 16384
LAYERS = 2
TILE = 128
NCHK = 8
GROUPS = 2
TILES_T = 64


def set_ends(values, rng, least, high):
    place = [jax.random.randint(jax.random.fold_in(rng, axis), (), 0, length) for axis, length in enumerate(values.shape)]
    main_axis = values.shape.index(max(values.shape))
    next_to = place[:main_axis] + [(place[main_axis] + 1) % values.shape[main_axis]] + place[main_axis + 1:]
    return values.at[tuple(place)].set(least).at[tuple(next_to)].set(high)


def with_spikes(array, key, source, target, shards_of, factor):
    owner, partner = [(jnp.arange(array.shape[dim]) // (array.shape[dim] // shards_of)).reshape([-1 if axis == dim else 1 for axis in range(array.ndim)]) for dim in (source, target)]
    chosen = jax.random.permutation(key, shards_of)[partner]
    strong = (owner == chosen) | (owner == (partner + shards_of // 2) % shards_of)
    return jnp.where(strong, factor * array, array)


def steps_of(own_key, shape, split, smallest, high):
    gain = 1.0
    for dim, parts in split:
        draws = jax.random.uniform(jax.random.fold_in(jax.random.fold_in(own_key, 6), dim), (parts,), jnp.float32, smallest / len(split), high / len(split))
        gain = gain * jnp.repeat(jnp.exp(draws), shape[dim] // parts).reshape((-1,) + (1,) * (len(shape) - 1 - dim))
    return gain


def bell_draw_with(rng, extent, width, most, split, heavy, dtype=jnp.bfloat16):
    values = width * jax.random.normal(rng, extent, jnp.float32)
    if split:
        values = values * steps_of(rng, extent, split, -0.22, 0.18)
    return jnp.clip(with_spikes(values, jax.random.fold_in(rng, 3), *heavy), -most, most).astype(dtype)


def setup_inputs(seed: int = 0) -> dict:
    arg_keys = jax.random.split(jax.random.key(seed), 4)
    master = bell_draw_with(arg_keys[0], (LAYERS, D, D), D ** -0.5, 0.09375, ((1, 32),), (1, 2, 32, 2.75), jnp.float32)
    tile_order = jax.vmap(lambda own: jax.random.permutation(own, TILES_T))(jax.random.split(arg_keys[1], GROUPS)).reshape((GROUPS, TILES_T)).astype(jnp.int32)
    check_weights = set_ends(jax.random.randint(arg_keys[2], (NCHK, D), -7, 8), jax.random.fold_in(arg_keys[2], 1), -7, 7).astype(jnp.int32)
    return dict(master=master, tile_order=tile_order, check_weights=check_weights)


def reference(master, tile_order, check_weights):
    low = master.astype(jnp.bfloat16)
    blocks = low.reshape(LAYERS, GROUPS, TILES_T, TILE, D)
    index = tile_order.astype(jnp.int32)[None, :, :, None, None]
    moved = jnp.take_along_axis(blocks, index, axis=2)
    tiled = moved.reshape(LAYERS, D, D)
    weights = check_weights.astype(jnp.bfloat16)
    sums = []
    for layer in range(LAYERS):
        sums.append(jnp.dot(weights, tiled[layer], preferred_element_type=jnp.float32))
    checksum = jnp.stack(sums, axis=0)
    return tiled, checksum
```

```python
import functools

import jax
import jax.numpy as jnp
from jax import lax
from jax.experimental import pallas as pl
from jax.experimental.pallas import tpu as pltpu
from jax.sharding import PartitionSpec as P

MESH = pl.DeviceIdType.MESH
TILE = 128
CHUNK = 64
GROUP = 8
VMEM = 58 * 2**20


def exchange_kernel(n, chunk, x, recv, stage, low, in_sem, own_sem, send_sem, recv_sem):
    layers, rows, _ = x.shape
    cols = recv.shape[2]
    per_layer = rows // chunk
    steps = layers * per_layer
    me = lax.axis_index("dp")
    other = lax.axis_index("tensor")

    barrier = pltpu.get_barrier_semaphore()

    def greet(s, carry):
        peer = lax.rem(me + s, n)
        pl.semaphore_signal(barrier, inc=1, device_id=(peer, other), device_id_type=MESH)
        return carry

    lax.fori_loop(1, n, greet, 0)

    def load(c):
        slot = lax.rem(c, 2)
        at = pl.multiple_of(lax.rem(c, per_layer) * chunk, chunk)
        return pltpu.make_async_copy(x.at[c // per_layer, pl.ds(at, chunk)], stage.at[slot], in_sem.at[slot])

    load(0).start()
    pl.semaphore_wait(barrier, n - 1)

    def step(c, carry):
        @pl.when(c + 1 < steps)
        def _():
            load(c + 1).start()

        load(c).wait()
        slot = lax.rem(c, 2)
        layer = c // per_layer
        at = pl.multiple_of(lax.rem(c, per_layer) * chunk, chunk)
        home = pl.multiple_of(me * rows + at, chunk)

        def one(i, carry):
            peer = lax.rem(me + lax.rem(i * 5, n), n)
            src = low.at[peer, layer, pl.ds(at, chunk)]
            src[...] = stage[slot, :, pl.ds(pl.multiple_of(peer * cols, cols), cols)].astype(jnp.bfloat16)

            @pl.when(i < n)
            def _():
                pltpu.make_async_remote_copy(
                    src_ref=src,
                    dst_ref=recv.at[layer, pl.ds(home, chunk)],
                    send_sem=send_sem.at[peer],
                    recv_sem=recv_sem.at[me],
                    device_id=(peer, other),
                    device_id_type=MESH,
                ).start()

            return carry

        lax.fori_loop(1, n + 1, one, 0)
        return carry

    lax.fori_loop(0, steps, step, 0)

    def place(p):
        return recv.at[:, pl.ds(pl.multiple_of(p * rows, rows), rows)]

    own = pltpu.make_async_copy(low.at[me], place(me), own_sem)
    own.start()

    def finish(s, carry):
        peer = lax.rem(me + s, n)
        pltpu.make_async_remote_copy(
            src_ref=low.at[peer],
            dst_ref=place(peer),
            send_sem=send_sem.at[peer],
            recv_sem=recv_sem.at[peer],
            device_id=(peer, other),
            device_id_type=MESH,
        ).wait()
        return carry

    lax.fori_loop(1, n, finish, 0)
    own.wait()


def exchange(n, x):
    layers, rows, width = x.shape
    cols = width // n
    chunk = min(CHUNK, rows)
    return pl.pallas_call(
        functools.partial(exchange_kernel, n, chunk),
        out_shape=jax.ShapeDtypeStruct((layers, n * rows, cols), jnp.bfloat16),
        in_specs=[pl.BlockSpec(memory_space=pl.ANY)],
        out_specs=pl.BlockSpec(memory_space=pl.ANY),
        scratch_shapes=[
            pltpu.VMEM((2, chunk, width), jnp.float32),
            pltpu.VMEM((n, layers, rows, cols), jnp.bfloat16),
            pltpu.SemaphoreType.DMA((2,)),
            pltpu.SemaphoreType.DMA,
            pltpu.SemaphoreType.DMA((n,)),
            pltpu.SemaphoreType.DMA((n,)),
        ],
        compiler_params=pltpu.CompilerParams(collective_id=0, has_side_effects=True, vmem_limit_bytes=VMEM),
        name="exchange",
    )(x)


def place_kernel(order, *refs):
    tiles, (weights, out, sums) = refs[:-3], refs[-3:]
    for i, tile in enumerate(tiles):
        out[0, i * TILE : (i + 1) * TILE, :] = tile[0]
    part = jnp.dot(weights[...], out[0], preferred_element_type=jnp.float32)

    @pl.when(pl.program_id(1) == 0)
    def _():
        sums[0] = part

    @pl.when(pl.program_id(1) > 0)
    def _():
        sums[0] += part


def place_tiles(order, received, weights):
    layers, rows, cols = received.shape
    checks = weights.shape[0]
    count = rows // TILE
    group = min(GROUP, count)

    def tile_at(i):
        return pl.BlockSpec((1, TILE, cols), lambda l, k, order: (l, order[k * group + i], 0))

    return pl.pallas_call(
        place_kernel,
        out_shape=(
            jax.ShapeDtypeStruct((layers, rows, cols), jnp.bfloat16),
            jax.ShapeDtypeStruct((layers, checks, cols), jnp.float32),
        ),
        grid_spec=pltpu.PrefetchScalarGridSpec(
            num_scalar_prefetch=1,
            grid=(layers, count // group),
            in_specs=[tile_at(i) for i in range(group)]
            + [pl.BlockSpec((checks, group * TILE), lambda l, k, order: (0, k))],
            out_specs=(
                pl.BlockSpec((1, group * TILE, cols), lambda l, k, order: (l, k, 0)),
                pl.BlockSpec((1, checks, cols), lambda l, k, order: (l, 0, 0)),
            ),
        ),
        compiler_params=pltpu.CompilerParams(vmem_limit_bytes=VMEM),
        name="place",
    )(order, *([received] * group), weights)


def on_device(n, owners, master, tile_order, check_weights):
    received = exchange(n, master)
    weights = check_weights.astype(jnp.bfloat16)
    tiled, part = place_tiles(tile_order[0], received, weights)
    me = lax.axis_index("tensor")
    width = part.shape[2] // owners

    def share(t):
        return lax.dynamic_slice_in_dim(part, t * width, width, axis=2)

    total = share(me)
    for s in range(1, owners):
        pairs = [(i, (i + s) % owners) for i in range(owners)]
        total += lax.ppermute(share(lax.rem(me + s, owners)), "tensor", pairs)
    return tiled, total


def solution(mesh):
    in_specs = (P(None, ("tensor", "dp"), None), P("tensor", None), P(None, "tensor"))
    out_specs = (P(None, "tensor", "dp"), P(None, None, ("dp", "tensor")))
    return jax.shard_map(
        functools.partial(on_device, mesh.shape["dp"], mesh.shape["tensor"]),
        mesh=mesh,
        in_specs=in_specs,
        out_specs=out_specs,
        check_vma=False,
    )
```

```python
import functools

import jax
import jax.numpy as jnp
from jax import lax
from jax.experimental import pallas as pl
from jax.experimental.pallas import tpu as pltpu
from jax.sharding import PartitionSpec as P

MESH = pl.DeviceIdType.MESH
TILE = 128
CHUNK = 64
GROUP = 16
VMEM = 58 * 2**20


def exchange_kernel(n, chunk, x, recv, stage, low, in_sem, own_sem, send_sem, recv_sem):
    layers, rows, _ = x.shape
    cols = recv.shape[2]
    per_layer = rows // chunk
    steps = layers * per_layer
    me = lax.axis_index("dp")
    other = lax.axis_index("tensor")

    barrier = pltpu.get_barrier_semaphore()

    def greet(s, carry):
        peer = lax.rem(me + s, n)
        pl.semaphore_signal(barrier, inc=1, device_id=(peer, other), device_id_type=MESH)
        return carry

    lax.fori_loop(1, n, greet, 0)

    def load(c):
        slot = lax.rem(c, 2)
        at = pl.multiple_of(lax.rem(c, per_layer) * chunk, chunk)
        return pltpu.make_async_copy(x.at[c // per_layer, pl.ds(at, chunk)], stage.at[slot], in_sem.at[slot])

    load(0).start()
    pl.semaphore_wait(barrier, n - 1)

    def step(c, carry):
        @pl.when(c + 1 < steps)
        def _():
            load(c + 1).start()

        load(c).wait()
        slot = lax.rem(c, 2)
        layer = c // per_layer
        at = pl.multiple_of(lax.rem(c, per_layer) * chunk, chunk)
        home = pl.multiple_of(me * rows + at, chunk)

        def one(i, carry):
            peer = lax.rem(me + lax.rem(i * 5, n), n)
            src = low.at[peer, layer, pl.ds(at, chunk)]
            src[...] = stage[slot, :, pl.ds(pl.multiple_of(peer * cols, cols), cols)].astype(jnp.bfloat16)

            @pl.when(i < n)
            def _():
                pltpu.make_async_remote_copy(
                    src_ref=src,
                    dst_ref=recv.at[layer, pl.ds(home, chunk)],
                    send_sem=send_sem.at[peer],
                    recv_sem=recv_sem.at[me],
                    device_id=(peer, other),
                    device_id_type=MESH,
                ).start()

            return carry

        lax.fori_loop(1, n + 1, one, 0)
        return carry

    lax.fori_loop(0, steps, step, 0)

    def place(p):
        return recv.at[:, pl.ds(pl.multiple_of(p * rows, rows), rows)]

    own = pltpu.make_async_copy(low.at[me], place(me), own_sem)
    own.start()

    def finish(s, carry):
        peer = lax.rem(me + s, n)
        pltpu.make_async_remote_copy(
            src_ref=low.at[peer],
            dst_ref=place(peer),
            send_sem=send_sem.at[peer],
            recv_sem=recv_sem.at[peer],
            device_id=(peer, other),
            device_id_type=MESH,
        ).wait()
        return carry

    lax.fori_loop(1, n, finish, 0)
    own.wait()


def exchange(n, x):
    layers, rows, width = x.shape
    cols = width // n
    chunk = min(CHUNK, rows)
    return pl.pallas_call(
        functools.partial(exchange_kernel, n, chunk),
        out_shape=jax.ShapeDtypeStruct((layers, n * rows, cols), jnp.bfloat16),
        in_specs=[pl.BlockSpec(memory_space=pl.ANY)],
        out_specs=pl.BlockSpec(memory_space=pl.ANY),
        scratch_shapes=[
            pltpu.VMEM((2, chunk, width), jnp.float32),
            pltpu.VMEM((n, layers, rows, cols), jnp.bfloat16),
            pltpu.SemaphoreType.DMA((2,)),
            pltpu.SemaphoreType.DMA,
            pltpu.SemaphoreType.DMA((n,)),
            pltpu.SemaphoreType.DMA((n,)),
        ],
        compiler_params=pltpu.CompilerParams(collective_id=0, has_side_effects=True, vmem_limit_bytes=VMEM),
        name="exchange",
    )(x)


def place_kernel(order, *refs):
    tiles, (weights, out, sums) = refs[:-3], refs[-3:]
    for i, tile in enumerate(tiles):
        out[0, i * TILE : (i + 1) * TILE, :] = tile[0]
    part = jnp.dot(weights[...], out[0], preferred_element_type=jnp.float32)

    @pl.when(pl.program_id(1) == 0)
    def _():
        sums[0] = part

    @pl.when(pl.program_id(1) > 0)
    def _():
        sums[0] += part


def place_tiles(order, received, weights):
    layers, rows, cols = received.shape
    checks = weights.shape[0]
    count = rows // TILE
    group = min(GROUP, count)

    def tile_at(i):
        return pl.BlockSpec((1, TILE, cols), lambda l, k, order: (l, order[k * group + i], 0))

    return pl.pallas_call(
        place_kernel,
        out_shape=(
            jax.ShapeDtypeStruct((layers, rows, cols), jnp.bfloat16),
            jax.ShapeDtypeStruct((layers, checks, cols), jnp.float32),
        ),
        grid_spec=pltpu.PrefetchScalarGridSpec(
            num_scalar_prefetch=1,
            grid=(layers, count // group),
            in_specs=[tile_at(i) for i in range(group)]
            + [pl.BlockSpec((checks, group * TILE), lambda l, k, order: (0, k))],
            out_specs=(
                pl.BlockSpec((1, group * TILE, cols), lambda l, k, order: (l, k, 0)),
                pl.BlockSpec((1, checks, cols), lambda l, k, order: (l, 0, 0)),
            ),
        ),
        compiler_params=pltpu.CompilerParams(vmem_limit_bytes=VMEM),
        name="place",
    )(order, *([received] * group), weights)


def on_device(n, owners, master, tile_order, check_weights):
    received = exchange(n, master)
    weights = check_weights.astype(jnp.bfloat16)
    tiled, part = place_tiles(tile_order[0], received, weights)
    me = lax.axis_index("tensor")
    width = part.shape[2] // owners

    def share(t):
        return lax.dynamic_slice_in_dim(part, t * width, width, axis=2)

    total = share(me)
    for s in range(1, owners):
        pairs = [(i, (i + s) % owners) for i in range(owners)]
        total += lax.ppermute(share(lax.rem(me + s, owners)), "tensor", pairs)
    return tiled, total


def solution(mesh):
    in_specs = (P(None, ("tensor", "dp"), None), P("tensor", None), P(None, "tensor"))
    out_specs = (P(None, "tensor", "dp"), P(None, None, ("dp", "tensor")))
    return jax.shard_map(
        functools.partial(on_device, mesh.shape["dp"], mesh.shape["tensor"]),
        mesh=mesh,
        in_specs=in_specs,
        out_specs=out_specs,
        check_vma=False,
    )
```
